32 devices in a mesh: expert: 4 (over y, x), replica: 8 (over z, core).
Axes of the slice: x: 2, y: 2, z: 4, core: 2. Of those that a mesh axis runs over, the one named last changes fastest.
Arguments:
- grad_out: bfloat16 [8, 2048, 2048], P('replica', 'expert'), may hold values from -6 to 6
- routes: int32 [8, 2048], P('replica', 'expert'), may hold values from 0 to 3, as said below
- hidden: bfloat16 [8, 2048, 768], P('replica', 'expert'), may hold values from -6 to 6
- weight: float32 [8, 4, 768, 2048], P('replica', 'expert'), may hold values from -6 to 6
- momentum: bfloat16 [8, 4, 768, 2048], P('replica', 'expert'), may hold values from -6 to 6
- probes: float32 [4, 4, 2048, 32], P('expert'), may hold values from -6 to 6
- pairing: int32 [4], replicated, may hold values from 1 to 7, as said below
Outputs:
- grad_hidden: bfloat16 [8, 2048, 768], P('replica', 'expert')
- new_momentum: bfloat16 [8, 4, 768, 2048], P('replica', 'expert')
- new_weight: float32 [8, 4, 768, 2048], P('replica', 'expert')
The draws below stay inside these ranges and needn't reach their ends.
Inputs may be any that keep to these rules, and one draw needn't show every extreme that they name: `routes`: in every replica, each block of 512 consecutive rows names every expert exactly 512 / 4 times. Round k pairs replica r with replica r XOR pairing[k]. Some round has pairing 8 / 2, some round has pairing 1 and some round has pairing 8 - 1.
All inputs are finite; a program needn't handle non-finite values.
Results may differ from the reference program's by a relative error of at most 0.0049.
Values may be sent and summed in bfloat16 or wider, within the bound.
A program may use at most 128 MiB of HBM per device.

```python
import math
import jax
import jax.numpy as jnp
from jax import lax

D = 2048
FF = 768
TOK_DEV = 512
RANK = 32
ROUNDS = 4
EXPERTS = 4
TOKENS = 2048
N_REPLICA = 8


def draw_routes(key, part):
    pattern = jnp.tile(jnp.arange(EXPERTS, dtype=jnp.int32), TOK_DEV // EXPERTS)
    key_list = jax.random.split(jax.random.fold_in(key, 17), N_REPLICA * EXPERTS)
    shuffled = jax.vmap(lambda sub_key: jax.random.permutation(sub_key, pattern))(key_list)
    return shuffled.reshape(N_REPLICA, TOKENS).astype(jnp.int32)


def draw_pairing(key, part):
    first_key, second_key = jax.random.split(jax.random.fold_in(key, 29))
    patterns = jax.random.randint(first_key, (ROUNDS,), 1, N_REPLICA).astype(jnp.int32)
    patterns = patterns.at[0].set(N_REPLICA // 2).at[1].set(1).at[2].set(N_REPLICA - 1)
    order = jax.random.permutation(second_key, ROUNDS)
    return patterns[order].astype(jnp.int32)


def levels(stream_key, dims, cuts, low, largest):
    loudness = 1.0
    for dim, blocks in cuts:
        draws = jax.random.uniform(jax.random.fold_in(jax.random.fold_in(stream_key, 6), dim), (blocks,), jnp.float32, low / len(cuts), largest / len(cuts))
        loudness = loudness * jnp.repeat(jnp.exp(draws), dims[dim] // blocks).reshape((-1,) + (1,) * (len(dims) - 1 - dim))
    return loudness


def noise(own_key, shape, spread, most, cuts=(), kind=jnp.bfloat16):
    loudness = levels(own_key, shape, cuts, -0.22, 0.18) if cuts else 1.0
    values = jax.random.normal(own_key, shape, jnp.float32) * spread * loudness
    return jnp.minimum(jnp.maximum(values, -most), most).astype(kind)


def setup_inputs(seed: int = 0) -> dict:
    splits = jax.random.split(jax.random.key(seed), 8)
    return {
        "grad_out": noise(splits[0], (N_REPLICA, TOKENS, D), 1.0, 6.0, ((0, 8), (1, 4))),
        "routes": draw_routes(jax.random.fold_in(splits[7], 71), 0),
        "hidden": noise(splits[2], (N_REPLICA, EXPERTS * TOK_DEV, FF), 1.0, 6.0, ((0, 8), (1, 4))),
        "weight": noise(splits[3], (N_REPLICA, EXPERTS, FF, D), 1.0, 6.0, ((0, 8), (1, 4)), jnp.float32),
        "momentum": noise(splits[4], (N_REPLICA, EXPERTS, FF, D), 1.0, 6.0, ((0, 8), (1, 4))),
        "probes": noise(splits[5], (EXPERTS, ROUNDS, D, RANK), 1.0, 6.0, ((0, 4),), jnp.float32),
        "pairing": draw_pairing(jax.random.fold_in(splits[7], 71), 0),
    }


learn_rate = 0.1
decay_rate = 0.9

def orthonormal(left_diff):
    gram_matrix = jnp.dot(left_diff, left_diff.T, precision=lax.Precision.HIGHEST)
    chol_factor = jnp.linalg.cholesky(gram_matrix)
    return jax.scipy.linalg.solve_triangular(chol_factor, left_diff, lower=True)

def reference(grad_out, routes, hidden, weight, momentum, probes, pairing):
    width_scale = 1.0 / math.sqrt(FF)
    per_peer = TOK_DEV // EXPERTS

    def one_replica(items):
        out_rows, route_ids, saved_acts, masters, moments = items
        blocks = out_rows.reshape(EXPERTS, TOK_DEV, D)
        ranking = jnp.argsort(route_ids.reshape(EXPERTS, TOK_DEV), axis=1, stable=True).astype(jnp.int32)
        sorted_rows = jnp.take_along_axis(blocks, ranking[:, :, None], axis=1)
        received = sorted_rows.reshape(EXPERTS, EXPERTS, per_peer, D).transpose(1, 0, 2, 3).reshape(EXPERTS, TOK_DEV, D)
        saved_acts = saved_acts.reshape(EXPERTS, TOK_DEV, FF)

        def one_expert(inner):
            got_rows, act_rows, master, old_moment = inner
            master_bf = master.astype(jnp.bfloat16)
            grad_in = lax.dot_general(got_rows.astype(jnp.float32), master_bf.astype(jnp.float32), (((1,), (1,)), ((), ())), preferred_element_type=jnp.float32)
            grad_in = (grad_in * width_scale).astype(jnp.bfloat16)
            grad_weight = lax.dot_general(act_rows.astype(jnp.float32), got_rows.astype(jnp.float32), (((0,), (0,)), ((), ())), preferred_element_type=jnp.float32) * width_scale
            moment = decay_rate * old_moment.astype(jnp.float32) + grad_weight
            return (grad_in, moment.astype(jnp.bfloat16), master - learn_rate * moment)
        return lax.map(one_expert, (received, saved_acts, masters, moments))
    grad_in, new_momentum, stepped = lax.map(one_replica, (grad_out, routes, hidden, weight, momentum))
    grad_in = grad_in.reshape(N_REPLICA, EXPERTS * TOK_DEV, FF)
    replicas = jnp.arange(N_REPLICA, dtype=jnp.int32)
    highest = lax.Precision.HIGHEST
    for round_index in range(ROUNDS):
        partner = jnp.bitwise_xor(replicas, pairing[round_index]).astype(jnp.int32)
        orient = jnp.where(replicas < partner, 1.0, -1.0).astype(jnp.float32)[:, None, None, None]
        own_left = jnp.einsum('edk,refd->rekf', probes[:, round_index], stepped, precision=highest)
        left_diff = orient * (own_left - own_left[partner])
        basis_rows = jax.vmap(jax.vmap(orthonormal))(left_diff)
        own_right = jnp.einsum('rekf,refd->rekd', basis_rows, stepped, precision=highest)
        right_diff = orient * (own_right - own_right[partner])
        stepped = stepped - 0.5 * orient * jnp.einsum('rekf,rekd->refd', basis_rows, right_diff, precision=highest)
    return (grad_in, new_momentum, stepped)
```

```python
import functools
import math

import jax
import jax.numpy as jnp
from jax import lax
from jax.experimental import pallas as pl
from jax.experimental.pallas import tpu as pltpu
from jax.sharding import PartitionSpec as P

learn_rate = 0.1
decay_rate = 0.9

BF = jnp.bfloat16
F32 = jnp.float32
VM = pltpu.CompilerParams(vmem_limit_bytes=32 * 2**20)

NN = (((1,), (0,)), ((), ()))
NT = (((1,), (1,)), ((), ()))
TN = (((0,), (0,)), ((), ()))


def dot(a, b, dims=NN):
    return lax.dot_general(a, b, dims, preferred_element_type=F32)


def sort_kernel(groups, routes_ref, rows_ref, out_ref, perm):
    rows = rows_ref.shape[0]

    @pl.when(pl.program_id(0) == 0)
    def _():
        width = max(8, groups)
        ids = lax.broadcasted_iota(jnp.int32, (width, rows), 0)
        named = ids == jnp.broadcast_to(routes_ref[...], (width, rows))
        before = lax.broadcasted_iota(jnp.int32, (rows, rows), 0) < lax.broadcasted_iota(
            jnp.int32, (rows, rows), 1
        )
        count = dot(
            jnp.where(named, 1.0, 0.0).astype(BF), jnp.where(before, 1.0, 0.0).astype(BF)
        )
        start = ids.astype(F32) * (rows // groups)
        place = jnp.sum(jnp.where(named, count + start, 0.0), axis=0, keepdims=True)
        slot = lax.broadcasted_iota(jnp.int32, (rows, rows), 0)
        hit = slot == jnp.broadcast_to(place.astype(jnp.int32), (rows, rows))
        perm[...] = jnp.where(hit, 1.0, 0.0).astype(BF)

    out_ref[...] = dot(perm[...], rows_ref[...]).astype(BF)


def sort_rows(routes, rows, groups):
    count, width = rows.shape
    cols = width // 4
    return pl.pallas_call(
        functools.partial(sort_kernel, groups),
        grid=(4,),
        in_specs=[
            pl.BlockSpec((1, count), lambda i: (0, 0)),
            pl.BlockSpec((count, cols), lambda i: (0, i)),
        ],
        out_specs=pl.BlockSpec((count, cols), lambda i: (0, i)),
        out_shape=jax.ShapeDtypeStruct((count, width), BF),
        scratch_shapes=[pltpu.VMEM((count, count), BF)],
        compiler_params=VM,
    )(routes, rows)


def step_kernel(scale, got_ref, act_ref, w_ref, m_ref, p_ref, gi_ref, nm_ref, a_ref, ab_ref, l_ref):
    got = got_ref[...]
    w = w_ref[...]
    gi_ref[...] = (dot(got, w.astype(BF), NT) * scale).astype(BF)
    moment = decay_rate * m_ref[...].astype(F32) + dot(act_ref[...], got, TN) * scale
    nm_ref[...] = moment.astype(BF)
    stepped = w - learn_rate * moment
    a_ref[...] = stepped
    ab = stepped.astype(BF)
    ab_ref[...] = ab
    l_ref[...] = dot(p_ref[...], ab, NT)


def step(got, act, weight, momentum, probes, ff_block):
    rows, width = got.shape
    ff = act.shape[2]
    np_ = probes.shape[0]
    fb = ff_block
    wide = pl.BlockSpec((None, None, fb, width), lambda i: (0, 0, i, 0))
    flat = pl.BlockSpec((fb, width), lambda i: (i, 0))
    return pl.pallas_call(
        functools.partial(step_kernel, 1.0 / math.sqrt(ff)),
        grid=(ff // fb,),
        in_specs=[
            pl.BlockSpec((rows, width), lambda i: (0, 0)),
            pl.BlockSpec((None, rows, fb), lambda i: (0, 0, i)),
            wide,
            wide,
            pl.BlockSpec((np_, width), lambda i: (0, 0)),
        ],
        out_specs=[
            pl.BlockSpec((None, rows, fb), lambda i: (0, 0, i)),
            wide,
            flat,
            flat,
            pl.BlockSpec((np_, fb), lambda i: (0, i)),
        ],
        out_shape=[
            jax.ShapeDtypeStruct((1, rows, ff), BF),
            jax.ShapeDtypeStruct((1, 1, ff, width), BF),
            jax.ShapeDtypeStruct((ff, width), F32),
            jax.ShapeDtypeStruct((ff, width), BF),
            jax.ShapeDtypeStruct((np_, ff), F32),
        ],
        compiler_params=VM,
    )(got, act, weight, momentum, probes)


def inverse_factor(gram):
    n = gram.shape[0]
    row = lax.broadcasted_iota(jnp.int32, (n, 2 * n), 0)
    col = lax.broadcasted_iota(jnp.int32, (n, 2 * n), 1)
    eye = jnp.where(col - n == row, 1.0, 0.0)
    work = jnp.concatenate([gram, eye[:, n:]], axis=1)
    row1 = row[:, :1]
    pivots = jnp.zeros((n, 1), F32)
    for k in range(n):
        line = work[k : k + 1, :]
        pivot = line[:, k : k + 1]
        column = work[:, k : k + 1]
        pivots = jnp.where(row1 == k, column, pivots)
        if k < n - 1:
            lower = jnp.where(row1 > k, column, 0.0)
            work = work - lower * (line * (1.0 / pivot))
    return work[:, n:] * lax.rsqrt(pivots)


def basis_kernel(done, own_ref, other_ref, ab_ref, *refs):
    q_refs, z_refs = refs[:done], refs[done : 2 * done]
    q_ref, r_ref = refs[2 * done :]
    diff = own_ref[...].astype(F32) - other_ref[...].astype(F32)
    gram = lax.dot_general(diff, diff, NT, precision=lax.Precision.HIGHEST)
    factor = inverse_factor(gram)
    basis = lax.dot_general(factor, diff, NN, precision=lax.Precision.HIGHEST)
    qb = basis.astype(BF)
    q_ref[...] = qb
    right = dot(qb, ab_ref[...])
    for q, z in zip(q_refs, z_refs):
        right = right - dot(dot(qb, q[...], NT).astype(BF), z[...])
    r_ref[...] = right.astype(BF)


def basis(own, other, ab, qs, zs):
    rank, ff = own.shape
    return pl.pallas_call(
        functools.partial(basis_kernel, len(qs)),
        out_shape=[
            jax.ShapeDtypeStruct((rank, ff), BF),
            jax.ShapeDtypeStruct((rank, ab.shape[1]), BF),
        ],
        compiler_params=VM,
    )(own, other, ab, *qs, *zs)


def next_kernel(done, own_ref, other_ref, p_ref, l_ref, *refs):
    q_refs, z_refs = refs[:done], refs[done : 2 * done - 1]
    z_ref, n_ref = refs[2 * done - 1 :]
    z = (0.5 * (own_ref[...].astype(F32) + other_ref[...].astype(F32))).astype(BF)
    z_ref[...] = z
    probe = p_ref[...]
    left = l_ref[...]
    for q, zz in zip(q_refs, [r[...] for r in z_refs] + [z]):
        left = left - dot(dot(probe, zz, NT).astype(BF), q[...])
    n_ref[...] = left.astype(BF)


def next_left(own, other, probes, left, index, qs, zs):
    rank, width = own.shape
    ff = left.shape[1]
    full = lambda a: pl.BlockSpec(a.shape, lambda i: (0,) * a.ndim)
    return pl.pallas_call(
        functools.partial(next_kernel, len(qs)),
        grid=(1,),
        in_specs=[
            full(own),
            full(other),
            pl.BlockSpec((rank, width), lambda i: (index, 0)),
            pl.BlockSpec((rank, ff), lambda i: (index, 0)),
            *[full(a) for a in (*qs, *zs)],
        ],
        out_specs=[
            pl.BlockSpec((rank, width), lambda i: (0, 0)),
            pl.BlockSpec((rank, ff), lambda i: (0, 0)),
        ],
        out_shape=[
            jax.ShapeDtypeStruct((rank, width), BF),
            jax.ShapeDtypeStruct((rank, ff), BF),
        ],
        compiler_params=VM,
    )(own, other, probes, left, *qs, *zs)


def last_kernel(done, a_ref, own_ref, other_ref, *refs):
    q_refs, z_refs = refs[:done], refs[done : 2 * done - 1]
    out_ref = refs[2 * done - 1]
    z = (0.5 * (own_ref[...].astype(F32) + other_ref[...].astype(F32))).astype(BF)
    zs = jnp.concatenate([r[...] for r in z_refs] + [z], axis=0)
    qs = jnp.concatenate([r[...] for r in q_refs], axis=0)
    out_ref[...] = a_ref[...] - dot(qs, zs, TN)


def last(stepped, own, other, qs, zs, ff_block):
    ff, width = stepped.shape
    rank = own.shape[0]
    fixed = pl.BlockSpec((rank, width), lambda i: (0, 0))
    return pl.pallas_call(
        functools.partial(last_kernel, len(qs)),
        grid=(ff // ff_block,),
        in_specs=[
            pl.BlockSpec((ff_block, width), lambda i: (i, 0)),
            fixed,
            fixed,
            *[pl.BlockSpec((rank, ff_block), lambda i: (0, i)) for _ in qs],
            *[fixed for _ in zs],
        ],
        out_specs=pl.BlockSpec((None, None, ff_block, width), lambda i: (0, 0, i, 0)),
        out_shape=jax.ShapeDtypeStruct((1, 1, ff, width), F32),
        compiler_params=VM,
    )(stepped, own, other, *qs, *zs)


def exchange(block, pattern):
    count = lax.axis_size("replica")

    def across(mask):
        return lambda value: lax.ppermute(
            value, "replica", [(i, i ^ mask) for i in range(count)]
        )

    return lax.switch(pattern - 1, [across(m) for m in range(1, count)], block)


def body(grad_out, routes, hidden, weight, momentum, probes, pairing):
    groups = lax.axis_size("expert")
    rows, width = grad_out.shape[1:]
    rounds, _, rank = probes.shape[1:]
    ff = hidden.shape[2]
    ff_block = 128 if ff % 128 == 0 else ff
    flat_probes = probes[0].transpose(0, 2, 1).reshape(rounds * rank, width).astype(BF)
    outgoing = sort_rows(routes, grad_out[0], groups).reshape(groups, rows // groups, width)
    received = lax.all_to_all(outgoing, "expert", split_axis=0, concat_axis=0, tiled=True)
    grad_in, new_momentum, stepped, stepped_bf, lefts = step(
        received.reshape(rows, width), hidden, weight, momentum, flat_probes, ff_block
    )
    qs, zs = [], []
    left = lefts[:rank].astype(BF)
    for k in range(rounds):
        other = exchange(left, pairing[k])
        q, right = basis(left, other, stepped_bf, qs, zs)
        qs.append(q)
        other_right = exchange(right, pairing[k])
        if k < rounds - 1:
            z, left = next_left(right, other_right, flat_probes, lefts, k + 1, qs, zs)
            zs.append(z)
    new_weight = last(stepped, right, other_right, qs, zs, ff_block)
    return grad_in, new_momentum, new_weight


def solution(mesh):
    return jax.shard_map(
        body,
        mesh=mesh,
        in_specs=(
            P("replica", "expert", None),
            P("replica", "expert"),
            P("replica", "expert", None),
            P("replica", "expert", None, None),
            P("replica", "expert", None, None),
            P("expert", None, None, None),
            P(),
        ),
        out_specs=(
            P("replica", "expert", None),
            P("replica", "expert", None, None),
            P("replica", "expert", None, None),
        ),
        check_vma=False,
    )
```

```python
import functools
import math

import jax
import jax.numpy as jnp
from jax import lax
from jax.experimental import pallas as pl
from jax.experimental.pallas import tpu as pltpu
from jax.sharding import PartitionSpec as P

learn_rate = 0.1
decay_rate = 0.9

BF = jnp.bfloat16
F32 = jnp.float32
VMEM_BYTES = 56 * 2**20
VM = pltpu.CompilerParams(vmem_limit_bytes=VMEM_BYTES)
MESH = pl.DeviceIdType.MESH

NN = (((1,), (0,)), ((), ()))
NT = (((1,), (1,)), ((), ()))
TN = (((0,), (0,)), ((), ()))


def dot(a, b, dims=NN):
    return lax.dot_general(a, b, dims, preferred_element_type=F32)


def route_kernel(groups, routes_ref, rows_ref, out_ref, perm, outgoing, send_sem, recv_sem):
    me = lax.axis_index("expert")
    rows = rows_ref.shape[0]
    per = rows // groups
    barrier = pltpu.get_barrier_semaphore()
    for i in range(1, groups):
        pl.semaphore_signal(
            barrier, inc=1, device_id={"expert": lax.rem(me + i, groups)}, device_id_type=MESH
        )
    width = max(8, groups)
    ids = lax.broadcasted_iota(jnp.int32, (width, rows), 0)
    named = ids == jnp.broadcast_to(routes_ref[...], (width, rows))
    before = lax.broadcasted_iota(jnp.int32, (rows, rows), 0) < lax.broadcasted_iota(
        jnp.int32, (rows, rows), 1
    )
    count = dot(jnp.where(named, 1.0, 0.0).astype(BF), jnp.where(before, 1.0, 0.0).astype(BF))
    start = ids.astype(F32) * per
    place = jnp.sum(jnp.where(named, count + start, 0.0), axis=0, keepdims=True)
    slot = lax.broadcasted_iota(jnp.int32, (rows, rows), 0)
    hit = slot == jnp.broadcast_to(place.astype(jnp.int32), (rows, rows))
    perm[...] = jnp.where(hit, 1.0, 0.0).astype(BF)
    pl.semaphore_wait(barrier, groups - 1)
    copies = []
    for i in [*range(groups - 1, 0, -1)]:
        peer = lax.rem(me + i, groups)
        pick = perm[pl.ds(pl.multiple_of(peer * per, per), per), :]
        outgoing[i - 1] = dot(pick, rows_ref[...]).astype(BF)
        copy = pltpu.make_async_remote_copy(
            src_ref=outgoing.at[i - 1],
            dst_ref=out_ref.at[me],
            send_sem=send_sem.at[i - 1],
            recv_sem=recv_sem.at[i - 1],
            device_id={"expert": peer},
            device_id_type=MESH,
        )
        copy.start()
        copies.append(copy)
    pick = perm[pl.ds(pl.multiple_of(me * per, per), per), :]
    out_ref[me] = dot(pick, rows_ref[...]).astype(BF)
    for copy in copies:
        copy.wait()


def route_rows(routes, rows, groups):
    count, width = rows.shape
    per = count // groups
    return pl.pallas_call(
        functools.partial(route_kernel, groups),
        in_specs=[pl.BlockSpec(memory_space=pltpu.VMEM)] * 2,
        out_specs=pl.BlockSpec(memory_space=pltpu.VMEM),
        out_shape=jax.ShapeDtypeStruct((groups, per, width), BF),
        scratch_shapes=[
            pltpu.VMEM((count, count), BF),
            pltpu.VMEM((groups - 1, per, width), BF),
            pltpu.SemaphoreType.DMA((groups - 1,)),
            pltpu.SemaphoreType.DMA((groups - 1,)),
        ],
        compiler_params=pltpu.CompilerParams(
            vmem_limit_bytes=VMEM_BYTES, collective_id=0, has_side_effects=True
        ),
    )(routes, rows)


def step_kernel(scale, rounds, got_ref, act_ref, w_ref, m_ref, *refs):
    p_refs = refs[:rounds]
    gi_ref, nm_ref, a_ref, ab_ref = refs[rounds : rounds + 4]
    l_refs = refs[rounds + 4 :]
    got = got_ref[...]
    w = w_ref[...]
    gi_ref[...] = (dot(got, w.astype(BF), NT) * scale).astype(BF)
    moment = decay_rate * m_ref[...].astype(F32) + dot(act_ref[...], got, TN) * scale
    nm_ref[...] = moment.astype(BF)
    stepped = w - learn_rate * moment
    a_ref[...] = stepped
    ab = stepped.astype(BF)
    ab_ref[...] = ab
    left = dot(jnp.concatenate([p[...] for p in p_refs], axis=0), ab, NT)
    rank = p_refs[0].shape[0]
    for k, l_ref in enumerate(l_refs):
        l_ref[...] = left[k * rank : (k + 1) * rank].astype(l_ref.dtype)


def step(got, act, weight, momentum, probes, fb):
    rows, width = got.shape
    ff = act.shape[2]
    rank = probes[0].shape[0]
    wide = pl.BlockSpec((None, None, fb, width), lambda i: (0, 0, i, 0))
    flat = pl.BlockSpec((fb, width), lambda i: (i, 0))
    return pl.pallas_call(
        functools.partial(step_kernel, 1.0 / math.sqrt(ff), len(probes)),
        grid=(ff // fb,),
        in_specs=[
            pl.BlockSpec((rows, width), lambda i: (0, 0)),
            pl.BlockSpec((None, rows, fb), lambda i: (0, 0, i)),
            wide,
            wide,
            *[pl.BlockSpec((rank, width), lambda i: (0, 0)) for _ in probes],
        ],
        out_specs=[
            pl.BlockSpec((None, rows, fb), lambda i: (0, 0, i)),
            wide,
            flat,
            flat,
            *[pl.BlockSpec((rank, fb), lambda i: (0, i)) for _ in probes],
        ],
        out_shape=[
            jax.ShapeDtypeStruct((1, rows, ff), BF),
            jax.ShapeDtypeStruct((1, 1, ff, width), BF),
            jax.ShapeDtypeStruct((ff, width), F32),
            jax.ShapeDtypeStruct((ff, width), BF),
            *[jax.ShapeDtypeStruct((rank, ff), F32 if k else BF) for k in range(len(probes))],
        ],
        compiler_params=VM,
    )(got, act, weight, momentum, *probes)


def inverse_factor(gram):
    n = gram.shape[0]
    row = lax.broadcasted_iota(jnp.int32, (n, 2 * n), 0)
    col = lax.broadcasted_iota(jnp.int32, (n, 2 * n), 1)
    eye = jnp.where(col - n == row, 1.0, 0.0)
    work = jnp.concatenate([gram, eye[:, n:]], axis=1)
    row1 = row[:, :1]
    pivots = jnp.zeros((n, 1), F32)
    for k in range(n):
        line = work[k : k + 1, :]
        pivot = line[:, k : k + 1]
        column = work[:, k : k + 1]
        pivots = jnp.where(row1 == k, column, pivots)
        if k < n - 1:
            lower = jnp.where(row1 > k, column, 0.0)
            work = work - lower * (line * (1.0 / pivot))
    return work[:, n:] * lax.rsqrt(pivots)


CHUNKS = 4


def round_kernel(mask, past, own_ref, p_ref, l_ref, ab_ref, *refs):
    y_refs, z_refs = refs[:past], refs[past : 2 * past]
    y_ref, z_ref, n_ref = refs[2 * past : 2 * past + 3]
    ab, got_left, out_right, got_right, ab_sem, send_sem, recv_sem = refs[2 * past + 3 :]
    load = pltpu.make_async_copy(ab_ref, ab, ab_sem)
    load.start()
    partner = me = lax.axis_index("replica")
    for bit in range(mask.bit_length()):
        if mask >> bit & 1:
            size = 1 << bit
            partner = partner + size * (1 - 2 * lax.rem(me // size, 2))
    where = {"replica": partner}
    barrier = pltpu.get_barrier_semaphore()
    pl.semaphore_signal(barrier, inc=1, device_id=where, device_id_type=MESH)
    pl.semaphore_wait(barrier, 1)

    def send(src, dst, index):
        copy = pltpu.make_async_remote_copy(
            src_ref=src,
            dst_ref=dst,
            send_sem=send_sem.at[index],
            recv_sem=recv_sem.at[index],
            device_id=where,
            device_id_type=MESH,
        )
        copy.start()
        return copy

    left_copy = send(own_ref, got_left, CHUNKS)
    ys = jnp.concatenate([r[...] for r in y_refs], axis=0)
    probe = p_ref[...]
    left = l_ref[...]
    for y, z in zip(y_refs, z_refs):
        left = left - dot(dot(probe, z[...], NT).astype(BF), y[...])
    load.wait()
    left_copy.wait()
    yb = (own_ref[...].astype(F32) - got_left[...].astype(F32)).astype(BF)
    y_ref[...] = yb
    cross = dot(yb, ys, NT).astype(BF)
    cols = ab.shape[1] // CHUNKS
    copies = []
    for c in range(CHUNKS):
        part = slice(c * cols, (c + 1) * cols)
        zs = jnp.concatenate([r[:, part] for r in z_refs], axis=0)
        right = dot(yb, ab[:, part]) - dot(cross, zs)
        out_right[c] = right.astype(BF)
        copies.append(send(out_right.at[c], got_right.at[c], c))
    factor = inverse_factor(dot(yb, yb, NT))
    half = 0.5 * lax.dot_general(factor, factor, TN, precision=lax.Precision.HIGHEST)
    follow = jnp.zeros((probe.shape[0], yb.shape[0]), F32)
    for c in range(CHUNKS):
        part = slice(c * cols, (c + 1) * cols)
        copies[c].wait()
        both = out_right[c].astype(F32) + got_right[c].astype(F32)
        z = lax.dot_general(half, both, NN, precision=lax.Precision.HIGHEST).astype(BF)
        z_ref[:, part] = z
        follow = follow + dot(probe[:, part], z, NT)
    n_ref[...] = (left - dot(follow.astype(BF), yb)).astype(BF)


def one_round(pattern, own, probe, left, stepped_bf, ys, zs):
    rank, ff = own.shape
    width = stepped_bf.shape[1]
    vmem = pl.BlockSpec(memory_space=pltpu.VMEM)

    def across(mask):
        return pl.pallas_call(
            functools.partial(round_kernel, mask, len(ys)),
            in_specs=[vmem] * 3 + [pl.BlockSpec(memory_space=pl.ANY)] + [vmem] * (2 * len(ys)),
            out_specs=[vmem] * 3,
            out_shape=[
                jax.ShapeDtypeStruct((rank, ff), BF),
                jax.ShapeDtypeStruct((rank, width), BF),
                jax.ShapeDtypeStruct((rank, ff), BF),
            ],
            scratch_shapes=[
                pltpu.VMEM((ff, width), BF),
                pltpu.VMEM((rank, ff), BF),
                pltpu.VMEM((CHUNKS, rank, width // CHUNKS), BF),
                pltpu.VMEM((CHUNKS, rank, width // CHUNKS), BF),
                pltpu.SemaphoreType.DMA,
                pltpu.SemaphoreType.DMA((CHUNKS + 1,)),
                pltpu.SemaphoreType.DMA((CHUNKS + 1,)),
            ],
            compiler_params=pltpu.CompilerParams(
                vmem_limit_bytes=VMEM_BYTES, collective_id=mask, has_side_effects=True
            ),
        )

    masks = range(1, lax.axis_size("replica"))
    return lax.switch(
        pattern - 1, [across(m) for m in masks], own, probe, left, stepped_bf, *ys, *zs
    )


def last_kernel(count, a_ref, *refs):
    out_ref = refs[2 * count]
    ys = jnp.concatenate([r[...] for r in refs[:count]], axis=0)
    zs = jnp.concatenate([r[...] for r in refs[count : 2 * count]], axis=0)
    out_ref[...] = a_ref[...] - dot(ys, zs, TN)


def last(stepped, ys, zs, ff_block):
    ff, width = stepped.shape
    rank = ys[0].shape[0]
    return pl.pallas_call(
        functools.partial(last_kernel, len(ys)),
        grid=(ff // ff_block,),
        in_specs=[
            pl.BlockSpec((ff_block, width), lambda i: (i, 0)),
            *[pl.BlockSpec((rank, ff_block), lambda i: (0, i)) for _ in ys],
            *[pl.BlockSpec((rank, width), lambda i: (0, 0)) for _ in zs],
        ],
        out_specs=pl.BlockSpec((None, None, ff_block, width), lambda i: (0, 0, i, 0)),
        out_shape=jax.ShapeDtypeStruct((1, 1, ff, width), F32),
        compiler_params=VM,
    )(stepped, *ys, *zs)


def body(grad_out, routes, hidden, weight, momentum, probes, pairing):
    groups = lax.axis_size("expert")
    rows, width = grad_out.shape[1:]
    rounds, _, rank = probes.shape[1:]
    ff = hidden.shape[2]
    ff_block = 128 if ff % 128 == 0 else ff
    flipped = [probes[0, k].T.astype(BF) for k in range(rounds)]
    received = route_rows(routes, grad_out[0], groups)
    grad_in, new_momentum, stepped, stepped_bf, *lefts = step(
        received.reshape(rows, width), hidden, weight, momentum, flipped, ff_block
    )
    no_y = jnp.zeros((rank, ff), BF)
    no_z = jnp.zeros((rank, width), BF)
    ys, zs = [], []
    left = lefts[0]
    for k in range(rounds):
        later = min(k + 1, rounds - 1)
        fill = rounds - 1 - k
        y, z, left = one_round(
            pairing[k],
            left,
            flipped[later],
            lefts[later],
            stepped_bf,
            ys + [no_y] * fill,
            zs + [no_z] * fill,
        )
        ys.append(y)
        zs.append(z)
    new_weight = last(stepped, ys, zs, ff_block)
    return grad_in, new_momentum, new_weight


def solution(mesh):
    return jax.shard_map(
        body,
        mesh=mesh,
        in_specs=(
            P("replica", "expert", None),
            P("replica", "expert"),
            P("replica", "expert", None),
            P("replica", "expert", None, None),
            P("replica", "expert", None, None),
            P("expert", None, None, None),
            P(),
        ),
        out_specs=(
            P("replica", "expert", None),
            P("replica", "expert", None, None),
            P("replica", "expert", None, None),
        ),
        check_vma=False,
    )
```

```python
import functools
import math

import jax
import jax.numpy as jnp
from jax import lax
from jax.experimental import pallas as pl
from jax.experimental.pallas import tpu as pltpu
from jax.sharding import PartitionSpec as P

learn_rate = 0.1
decay_rate = 0.9

BF = jnp.bfloat16
F32 = jnp.float32
VMEM_BYTES = 56 * 2**20
VM = pltpu.CompilerParams(vmem_limit_bytes=VMEM_BYTES)
MESH = pl.DeviceIdType.MESH

NN = (((1,), (0,)), ((), ()))
NT = (((1,), (1,)), ((), ()))
TN = (((0,), (0,)), ((), ()))


def dot(a, b, dims=NN):
    return lax.dot_general(a, b, dims, preferred_element_type=F32)


def route_kernel(groups, routes_ref, rows_ref, out_ref, perm, outgoing, send_sem, recv_sem):
    me = lax.axis_index("expert")
    rows = rows_ref.shape[0]
    per = rows // groups
    barrier = pltpu.get_barrier_semaphore()
    for i in range(1, groups):
        pl.semaphore_signal(
            barrier, inc=1, device_id={"expert": lax.rem(me + i, groups)}, device_id_type=MESH
        )
    width = max(8, groups)
    ids = lax.broadcasted_iota(jnp.int32, (width, rows), 0)
    named = ids == jnp.broadcast_to(routes_ref[...], (width, rows))
    before = lax.broadcasted_iota(jnp.int32, (rows, rows), 0) < lax.broadcasted_iota(
        jnp.int32, (rows, rows), 1
    )
    count = dot(jnp.where(named, 1.0, 0.0).astype(BF), jnp.where(before, 1.0, 0.0).astype(BF))
    start = ids.astype(F32) * per
    place = jnp.sum(jnp.where(named, count + start, 0.0), axis=0, keepdims=True)
    slot = lax.broadcasted_iota(jnp.int32, (rows, rows), 0)
    hit = slot == jnp.broadcast_to(place.astype(jnp.int32), (rows, rows))
    perm[...] = jnp.where(hit, 1.0, 0.0).astype(BF)
    pl.semaphore_wait(barrier, groups - 1)
    copies = []
    for i in [*range(groups - 1, 0, -1)]:
        peer = lax.rem(me + i, groups)
        pick = perm[pl.ds(pl.multiple_of(peer * per, per), per), :]
        outgoing[i - 1] = dot(pick, rows_ref[...]).astype(BF)
        copy = pltpu.make_async_remote_copy(
            src_ref=outgoing.at[i - 1],
            dst_ref=out_ref.at[me],
            send_sem=send_sem.at[i - 1],
            recv_sem=recv_sem.at[i - 1],
            device_id={"expert": peer},
            device_id_type=MESH,
        )
        copy.start()
        copies.append(copy)
    pick = perm[pl.ds(pl.multiple_of(me * per, per), per), :]
    out_ref[me] = dot(pick, rows_ref[...]).astype(BF)
    for copy in copies:
        copy.wait()


def route_rows(routes, rows, groups):
    count, width = rows.shape
    per = count // groups
    return pl.pallas_call(
        functools.partial(route_kernel, groups),
        in_specs=[pl.BlockSpec(memory_space=pltpu.VMEM)] * 2,
        out_specs=pl.BlockSpec(memory_space=pltpu.VMEM),
        out_shape=jax.ShapeDtypeStruct((groups, per, width), BF),
        scratch_shapes=[
            pltpu.VMEM((count, count), BF),
            pltpu.VMEM((groups - 1, per, width), BF),
            pltpu.SemaphoreType.DMA((groups - 1,)),
            pltpu.SemaphoreType.DMA((groups - 1,)),
        ],
        compiler_params=pltpu.CompilerParams(
            vmem_limit_bytes=VMEM_BYTES, collective_id=0, has_side_effects=True
        ),
    )(routes, rows)


def step_kernel(scale, got_ref, act_ref, w_ref, m_ref, p_ref, *refs):
    gi_ref, nm_ref, a_ref, ab_ref = refs[:4]
    l_refs = refs[4:]
    rounds, rank, width = p_ref.shape
    got = got_ref[...]
    w = w_ref[...]
    gi_ref[...] = (dot(got, w.astype(BF), NT) * scale).astype(BF)
    moment = decay_rate * m_ref[...].astype(F32) + dot(act_ref[...], got, TN) * scale
    nm_ref[...] = moment.astype(BF)
    stepped = w - learn_rate * moment
    a_ref[...] = stepped
    ab = stepped.astype(BF)
    ab_ref[...] = ab
    left = dot(p_ref[...].reshape(rounds * rank, width).astype(BF), ab, NT)
    for k, l_ref in enumerate(l_refs):
        l_ref[...] = left[k * rank : (k + 1) * rank].astype(l_ref.dtype)


def step(got, act, weight, momentum, probes, fb):
    rows, width = got.shape
    ff = act.shape[2]
    rounds, rank, _ = probes.shape
    wide = pl.BlockSpec((None, None, fb, width), lambda i: (0, 0, i, 0))
    flat = pl.BlockSpec((fb, width), lambda i: (i, 0))
    return pl.pallas_call(
        functools.partial(step_kernel, 1.0 / math.sqrt(ff)),
        grid=(ff // fb,),
        in_specs=[
            pl.BlockSpec((rows, width), lambda i: (0, 0)),
            pl.BlockSpec((None, rows, fb), lambda i: (0, 0, i)),
            wide,
            wide,
            pl.BlockSpec((rounds, rank, width), lambda i: (0, 0, 0)),
        ],
        out_specs=[
            pl.BlockSpec((None, rows, fb), lambda i: (0, 0, i)),
            wide,
            flat,
            flat,
            *[pl.BlockSpec((rank, fb), lambda i: (0, i))] * rounds,
        ],
        out_shape=[
            jax.ShapeDtypeStruct((1, rows, ff), BF),
            jax.ShapeDtypeStruct((1, 1, ff, width), BF),
            jax.ShapeDtypeStruct((ff, width), F32),
            jax.ShapeDtypeStruct((ff, width), BF),
            *[jax.ShapeDtypeStruct((rank, ff), F32 if k else BF) for k in range(rounds)],
        ],
        compiler_params=VM,
    )(got, act, weight, momentum, probes)


def inverse_factor(gram):
    n = gram.shape[0]
    row = lax.broadcasted_iota(jnp.int32, (n, 2 * n), 0)
    col = lax.broadcasted_iota(jnp.int32, (n, 2 * n), 1)
    eye = jnp.where(col - n == row, 1.0, 0.0)
    work = jnp.concatenate([gram, eye[:, n:]], axis=1)
    row1 = row[:, :1]
    pivots = jnp.zeros((n, 1), F32)
    for k in range(n):
        line = work[k : k + 1, :]
        pivot = line[:, k : k + 1]
        column = work[:, k : k + 1]
        pivots = jnp.where(row1 == k, column, pivots)
        if k < n - 1:
            lower = jnp.where(row1 > k, column, 0.0)
            work = work - lower * (line * (1.0 / pivot))
    return work[:, n:] * lax.rsqrt(pivots)


CHUNKS = 4


def round_kernel(mask, past, final, own_ref, ab_ref, *refs):
    y_refs, z_refs = refs[:past], refs[past : 2 * past]
    refs = refs[2 * past :]
    if final:
        y_ref, z_ref = refs[:2]
        refs = refs[2:]
    else:
        p_ref, l_ref, y_ref, z_ref, n_ref = refs[:5]
        refs = refs[5:]
    ab, got_left, out_right, got_right, ab_sem, send_sem, recv_sem = refs
    load = pltpu.make_async_copy(ab_ref, ab, ab_sem)
    load.start()
    partner = me = lax.axis_index("replica")
    for bit in range(mask.bit_length()):
        if mask >> bit & 1:
            size = 1 << bit
            partner = partner + size * (1 - 2 * lax.rem(me // size, 2))
    where = {"replica": partner}
    barrier = pltpu.get_barrier_semaphore()
    pl.semaphore_signal(barrier, inc=1, device_id=where, device_id_type=MESH)
    pl.semaphore_wait(barrier, 1)

    def send(src, dst, index):
        copy = pltpu.make_async_remote_copy(
            src_ref=src,
            dst_ref=dst,
            send_sem=send_sem.at[index],
            recv_sem=recv_sem.at[index],
            device_id=where,
            device_id_type=MESH,
        )
        copy.start()
        return copy

    left_copy = send(own_ref, got_left, CHUNKS)
    if past:
        ys = jnp.concatenate([r[...] for r in y_refs], axis=0)
    if not final:
        probe = p_ref[...].astype(BF)
        left = l_ref[...]
        for y, z in zip(y_refs, z_refs):
            left = left - dot(dot(probe, z[...], NT).astype(BF), y[...])
        follow = jnp.zeros((probe.shape[0], own_ref.shape[0]), F32)
    load.wait()
    left_copy.wait()
    yb = (own_ref[...].astype(F32) - got_left[...].astype(F32)).astype(BF)
    y_ref[...] = yb
    if past:
        cross = dot(yb, ys, NT).astype(BF)
    cols = ab.shape[1] // CHUNKS
    copies = []
    for c in range(CHUNKS):
        part = slice(c * cols, (c + 1) * cols)
        right = dot(yb, ab[:, part])
        if past:
            zs = jnp.concatenate([r[:, part] for r in z_refs], axis=0)
            right = right - dot(cross, zs)
        out_right[c] = right.astype(BF)
        copies.append(send(out_right.at[c], got_right.at[c], c))
    factor = inverse_factor(dot(yb, yb, NT))
    half = 0.5 * lax.dot_general(factor, factor, TN, precision=lax.Precision.HIGHEST)
    for c in range(CHUNKS):
        part = slice(c * cols, (c + 1) * cols)
        copies[c].wait()
        both = out_right[c].astype(F32) + got_right[c].astype(F32)
        z = lax.dot_general(half, both, NN, precision=lax.Precision.HIGHEST).astype(BF)
        z_ref[:, part] = z
        if not final:
            follow = follow + dot(probe[:, part], z, NT)
    if not final:
        n_ref[...] = (left - dot(follow.astype(BF), yb)).astype(BF)


def one_round(pattern, index, own, probes, lefts, stepped_bf, ys, zs):
    rank, ff = own.shape
    width = stepped_bf.shape[1]
    vmem = pl.BlockSpec(memory_space=pltpu.VMEM)
    final = index + 1 == probes.shape[0]
    masks = range(1, lax.axis_size("replica"))
    follow = [] if final else [probes, lefts[index + 1]]
    probe_spec = pl.BlockSpec((None, rank, width), lambda i: (index + 1, 0, 0))

    def across(mask):
        return pl.pallas_call(
            functools.partial(round_kernel, mask, len(ys), final),
            grid=(1,),
            in_specs=[
                vmem,
                pl.BlockSpec(memory_space=pl.ANY),
                *[vmem] * (2 * len(ys)),
                *[probe_spec, vmem][: len(follow)],
            ],
            out_specs=[vmem] * (2 if final else 3),
            out_shape=[
                jax.ShapeDtypeStruct((rank, ff), BF),
                jax.ShapeDtypeStruct((rank, width), BF),
                jax.ShapeDtypeStruct((rank, ff), BF),
            ][: 2 if final else 3],
            scratch_shapes=[
                pltpu.VMEM((ff, width), BF),
                pltpu.VMEM((rank, ff), BF),
                pltpu.VMEM((CHUNKS, rank, width // CHUNKS), BF),
                pltpu.VMEM((CHUNKS, rank, width // CHUNKS), BF),
                pltpu.SemaphoreType.DMA,
                pltpu.SemaphoreType.DMA((CHUNKS + 1,)),
                pltpu.SemaphoreType.DMA((CHUNKS + 1,)),
            ],
            compiler_params=pltpu.CompilerParams(
                vmem_limit_bytes=VMEM_BYTES,
                collective_id=index * len(masks) + mask,
                has_side_effects=True,
            ),
        )

    return lax.switch(
        pattern - 1, [across(m) for m in masks], own, stepped_bf, *ys, *zs, *follow
    )


def last_kernel(count, a_ref, *refs):
    out_ref = refs[2 * count]
    ys = jnp.concatenate([r[...] for r in refs[:count]], axis=0)
    zs = jnp.concatenate([r[...] for r in refs[count : 2 * count]], axis=0)
    out_ref[...] = a_ref[...] - dot(ys, zs, TN)


def last(stepped, ys, zs, ff_block):
    ff, width = stepped.shape
    rank = ys[0].shape[0]
    return pl.pallas_call(
        functools.partial(last_kernel, len(ys)),
        grid=(ff // ff_block,),
        in_specs=[
            pl.BlockSpec((ff_block, width), lambda i: (i, 0)),
            *[pl.BlockSpec((rank, ff_block), lambda i: (0, i)) for _ in ys],
            *[pl.BlockSpec((rank, width), lambda i: (0, 0)) for _ in zs],
        ],
        out_specs=pl.BlockSpec((None, None, ff_block, width), lambda i: (0, 0, i, 0)),
        out_shape=jax.ShapeDtypeStruct((1, 1, ff, width), F32),
        compiler_params=VM,
    )(stepped, *ys, *zs)


def body(grad_out, routes, hidden, weight, momentum, probes, pairing):
    groups = lax.axis_size("expert")
    rows, width = grad_out.shape[1:]
    rounds, _, rank = probes.shape[1:]
    ff = hidden.shape[2]
    ff_block = 128 if ff % 128 == 0 else ff
    flipped = probes[0].transpose(0, 2, 1)
    received = route_rows(routes, grad_out[0], groups)
    grad_in, new_momentum, stepped, stepped_bf, *lefts = step(
        received.reshape(rows, width), hidden, weight, momentum, flipped, ff_block
    )
    ys, zs = [], []
    left = lefts[0]
    for k in range(rounds):
        y, z, *rest = one_round(pairing[k], k, left, flipped, lefts, stepped_bf, ys, zs)
        left = rest[0] if rest else None
        ys.append(y)
        zs.append(z)
    new_weight = last(stepped, ys, zs, ff_block)
    return grad_in, new_momentum, new_weight


def solution(mesh):
    return jax.shard_map(
        body,
        mesh=mesh,
        in_specs=(
            P("replica", "expert", None),
            P("replica", "expert"),
            P("replica", "expert", None),
            P("replica", "expert", None, None),
            P("replica", "expert", None, None),
            P("expert", None, None, None),
            P(),
        ),
        out_specs=(
            P("replica", "expert", None),
            P("replica", "expert", None, None),
            P("replica", "expert", None, None),
        ),
        check_vma=False,
    )
```
